256 devices in a mesh: batch: 256 (over y, z, x, core).
Axes of the slice: x: 4, y: 4, z: 8, core: 2. Of those that a mesh axis runs over, the one named last changes fastest.
Arguments:
- image: bfloat16 [32768, 1024], P('batch'), may hold values from -6 to 6
- text: bfloat16 [32768, 1024], P('batch'), may hold values from -6 to 6
- image_bank: bfloat16 [2048, 1024], P('batch'), may hold values from -6 to 6
- text_bank: bfloat16 [2048, 1024], P('batch'), may hold values from -6 to 6
Outputs:
- losses: float32 [6], replicated
- grad_image: float32 [32768, 1024], P('batch')
- grad_text: float32 [32768, 1024], P('batch')
- grad_image_bank: float32 [2048, 1024], P('batch')
- grad_text_bank: float32 [2048, 1024], P('batch')
The draws below stay inside these ranges and needn't reach their ends.
All inputs are finite; a program needn't handle non-finite values.
Results may differ from the reference program's by a relative error of at most 0.0033.
Values may be sent and summed in bfloat16 or wider, within the bound.
No kernel may reach another device: no remote copies, remote signals or barrier semaphores. Data moves between devices by JAX's collectives and lax.ppermute only.
A program may use at most 192 MiB of HBM per device.

```python
import jax
import jax.numpy as jnp
from jax import lax

D = 1024
ROWS = 128
QUERIES = 32768
BANK = 2048


def level_of(stream_key, shape, split, smallest, top_value):
    def one(position, parts):
        draws = jax.random.uniform(jax.random.fold_in(jax.random.fold_in(stream_key, 6), position), (parts,), jnp.float32, smallest / len(split), top_value / len(split))
        return jnp.repeat(jnp.exp(draws), shape[position] // parts).reshape((-1,) + (1,) * (len(shape) - position - 1))

    loudness = one(*split[0])
    for cut in split[1:]:
        loudness = loudness * one(*cut)
    return loudness


def bell_draw(key, dims, deviation, limit, shards=(), dtype=jnp.bfloat16):
    entries = jax.random.normal(key, dims, jnp.float32) * deviation
    if len(shards) > 0:
        entries = level_of(key, dims, shards, -0.22, 0.18) * entries
    return jnp.clip(entries, min=-limit, max=limit).astype(dtype)


def setup_inputs(seed: int = 0) -> dict:
    splits = jax.random.split(jax.random.key(seed), 5)
    image = bell_draw(splits[0], (QUERIES, D), 1.0, 6.0, ((0, 256),))
    text = bell_draw(splits[1], (QUERIES, D), 1.0, 6.0, ((0, 256),))
    image_bank = bell_draw(splits[2], (BANK, D), 1.0, 6.0, ((0, 256),))
    text_bank = bell_draw(splits[3], (BANK, D), 1.0, 6.0, ((0, 256),))
    return {"image": image, "text": text, "image_bank": image_bank, "text_bank": text_bank}


SCALE = 20.0
EPS = 1e-06

def inverse_norm(values, width):
    part = values[:, :width].astype(jnp.float32)
    return lax.rsqrt(lax.optimization_barrier(jnp.sum(part * part, axis=1)) + EPS)

def logits_block(query, rquery, keys, rkeys, width):
    dots = jnp.dot(query[:, :width], keys[:, :width].T, preferred_element_type=jnp.float32)
    return SCALE * dots * rquery[:, None] * rkeys[None, :]

def across_rows(left, right):
    return lax.dot_general(left, right, (((0,), (0,)), ((), ())), preferred_element_type=jnp.float32)

def level_terms(image, text, image_bank, text_bank, width):
    total, depth = image.shape
    blocks = total // ROWS
    banks = image_bank.shape[0]
    rimage_bank = inverse_norm(image_bank, width)
    rtext_bank = inverse_norm(text_bank, width)
    rimage = inverse_norm(image, width).reshape(blocks, ROWS)
    rtext = inverse_norm(text, width).reshape(blocks, ROWS)
    image_blocks = image.reshape(blocks, ROWS, depth)
    text_blocks = text.reshape(blocks, ROWS, depth)

    def step(carry, args):
        acc_image_bank, acc_text_bank, col_a, col_b = carry
        img, txt, rimg, rtxt = args
        img_wide = img[:, :width].astype(jnp.float32)
        txt_wide = txt[:, :width].astype(jnp.float32)
        matched = SCALE * lax.optimization_barrier(jnp.sum(img_wide * txt_wide, axis=1)) * rimg * rtxt
        scores_a = logits_block(img, rimg, text_bank, rtext_bank, width)
        scores_b = logits_block(txt, rtxt, image_bank, rimage_bank, width)
        lse_a = jnp.log(jnp.exp(matched) + lax.optimization_barrier(jnp.sum(jnp.exp(scores_a), axis=1)))
        lse_b = jnp.log(jnp.exp(matched) + lax.optimization_barrier(jnp.sum(jnp.exp(scores_b), axis=1)))
        probs_a = jnp.exp(scores_a - lse_a[:, None])
        probs_b = jnp.exp(scores_b - lse_b[:, None])
        match_grad = jnp.exp(matched - lse_a) + jnp.exp(matched - lse_b) - 2.0
        across_a = lax.optimization_barrier(jnp.sum(probs_a * scores_a, axis=1)) + match_grad * matched
        across_b = lax.optimization_barrier(jnp.sum(probs_b * scores_b, axis=1)) + match_grad * matched
        weights_a = (SCALE * rimg[:, None] * rtext_bank[None, :] * probs_a).astype(jnp.bfloat16)
        weights_b = (SCALE * rtxt[:, None] * rimage_bank[None, :] * probs_b).astype(jnp.bfloat16)
        cross = SCALE * match_grad * rimg * rtxt
        grad_img = jnp.dot(weights_a, text_bank[:, :width], preferred_element_type=jnp.float32) + cross[:, None] * txt_wide - (across_a * rimg * rimg)[:, None] * img_wide
        grad_txt = jnp.dot(weights_b, image_bank[:, :width], preferred_element_type=jnp.float32) + cross[:, None] * img_wide - (across_b * rtxt * rtxt)[:, None] * txt_wide
        acc_text_bank = acc_text_bank + across_rows(weights_a, img[:, :width])
        acc_image_bank = acc_image_bank + across_rows(weights_b, txt[:, :width])
        col_a = col_a + lax.optimization_barrier(jnp.sum(probs_a * scores_a, axis=0))
        col_b = col_b + lax.optimization_barrier(jnp.sum(probs_b * scores_b, axis=0))
        loss_part = jnp.sum(lse_a + lse_b - 2.0 * matched)
        return ((acc_image_bank, acc_text_bank, col_a, col_b), (grad_img, grad_txt, loss_part))
    start = (jnp.zeros((banks, width), jnp.float32), jnp.zeros((banks, width), jnp.float32), jnp.zeros((banks,), jnp.float32), jnp.zeros((banks,), jnp.float32))
    carry, outs = lax.scan(step, start, (image_blocks, text_blocks, rimage, rtext))
    acc_image_bank, acc_text_bank, col_a, col_b = carry
    grad_img, grad_txt, loss_parts = outs
    term_text_bank = acc_text_bank - (col_a * rtext_bank * rtext_bank)[:, None] * text_bank[:, :width].astype(jnp.float32)
    term_image_bank = acc_image_bank - (col_b * rimage_bank * rimage_bank)[:, None] * image_bank[:, :width].astype(jnp.float32)
    loss = jnp.sum(loss_parts) / (2.0 * total)
    return (loss, grad_img.reshape(total, width), grad_txt.reshape(total, width), term_image_bank, term_text_bank)

def reference(image, text, image_bank, text_bank):
    total, depth = image.shape
    banks = image_bank.shape[0]
    grad_image = jnp.zeros((total, depth), jnp.float32)
    grad_text = jnp.zeros((total, depth), jnp.float32)
    grad_image_bank = jnp.zeros((banks, depth), jnp.float32)
    grad_text_bank = jnp.zeros((banks, depth), jnp.float32)
    results = []
    for level in range(6):
        width = depth // 2 ** (5 - level)
        loss, grad_img, grad_txt, term_ib, term_tb = level_terms(image, text, image_bank, text_bank, width)
        results.append(loss)
        grad_image = grad_image.at[:, :width].add(grad_img)
        grad_text = grad_text.at[:, :width].add(grad_txt)
        grad_image_bank = grad_image_bank.at[:, :width].add(term_ib)
        grad_text_bank = grad_text_bank.at[:, :width].add(term_tb)
    return (jnp.stack(results), grad_image, grad_text, grad_image_bank, grad_text_bank)
```

```python
import jax
import jax.numpy as jnp
from jax import lax
from jax.experimental import pallas as pl
from jax.experimental.pallas import tpu as pltpu
from jax.sharding import Mesh, PartitionSpec as P

SCALE = 20.0
EPS = 1e-06
LOG2E = 1.4426950408889634
LEVELS = 6
EDGES = (0, 32, 64, 128, 256, 512, 1024)
D = 1024
ROWS = 128
RING = 4
CHUNK = ROWS * RING
QUERIES = 2 * CHUNK
KEYS = 256
LANES = 128
PAIRS = 32
STEP_F = 32
STEP_B = 32
VMEM_LIMIT = 56 * 1024 * 1024
BF = jnp.bfloat16
F32 = jnp.float32


def dot_nt(left, right):
    return lax.dot_general(left, right, (((1,), (1,)), ((), ())), preferred_element_type=F32)


def dot_nn(left, right):
    return lax.dot_general(left, right, (((1,), (0,)), ((), ())), preferred_element_type=F32)


def dot_tn(left, right):
    return lax.dot_general(left, right, (((0,), (0,)), ((), ())), preferred_element_type=F32)


def iota(shape, axis):
    return lax.broadcasted_iota(jnp.int32, shape, axis)


def level_mask(shape, level_axis):
    width = jnp.left_shift(32, jnp.minimum(iota(shape, level_axis), LEVELS - 1))
    return jnp.where(iota(shape, 1 - level_axis) < width, 1.0, 0.0).astype(BF)


def halves(values):
    high = values.astype(BF)
    return high, (values - high.astype(F32)).astype(BF)


def sums_across(values, mask):
    high, low = halves(values)
    return dot_nt(mask, high) + dot_nt(mask, low)


def sums_down(values, mask):
    high, low = halves(values)
    return dot_nn(high, mask) + dot_nn(low, mask)


def pick_lanes(values, level):
    lane = iota(values.shape, 1)
    keep = (lane >= EDGES[level]) & (lane < EDGES[level + 1])
    return jnp.where(keep, values.astype(F32), 0.0).astype(BF)


def keys_of(keys, side):
    return slice((1 - side) * D, (2 - side) * D)


def raw_scores(keys, queries, dots, side):
    base = (1 - side) * D
    for level in range(3):
        dots[level] = dot_nt(keys[:, base : base + LANES], pick_lanes(queries[side, :, :LANES], level))
    for level in range(3, LEVELS):
        lower, upper = EDGES[level], EDGES[level + 1]
        dots[level] = dot_nt(keys[:, base + lower : base + upper], queries[side, :, lower:upper])


def fold(values):
    return jnp.sum(values.reshape(values.shape[0] // 8, 8, values.shape[1]), axis=0)


def widen(values, n):
    return jnp.concatenate([values] * n, axis=1)


def spread(cols, level):
    return jnp.broadcast_to(cols[:, level : level + 1], (cols.shape[0], LANES))


def prepare(q0, q1, q2, q3, late, xs, rq, matched):
    across = level_mask((16, D), 0)
    for side in range(2):
        for s, q in enumerate((q0, q1, q2, q3)):
            xs[side, s * ROWS : (s + 1) * ROWS, :] = q[side * ROWS : (side + 1) * ROWS, :]
        wide = xs[side].astype(F32)
        rq[side] = lax.rsqrt(sums_across(wide * wide, across) + EPS)[:8]
    product = q0[:ROWS, :].astype(F32) * q0[ROWS:, :].astype(F32)
    matched[...] = SCALE * sums_across(product, across)[:8] * rq[0, :, :ROWS] * rq[1, :, :ROWS]


def forward(xs, xo, rq, ro, matched, keys, sums, kn, dots, wide):
    down = level_mask((D, LANES), 1)
    grown = jnp.exp(matched[...])
    for side in range(2):
        y = keys[:, keys_of(keys, side)].astype(F32)
        norms = lax.rsqrt(sums_down(y * y, down) + EPS)
        kn[side] = norms
        for level in range(LEVELS):
            wide[level] = spread(norms, level)
        for part, (queries, scale) in enumerate(((xs, rq), (xo, ro))):
            raw_scores(keys, queries, dots, side)
            row = (SCALE * LOG2E) * scale[side]

            def body(t, acc):
                at = pl.ds(pl.multiple_of(t * STEP_F, STEP_F), STEP_F)
                dot = jnp.zeros((STEP_F, CHUNK), F32)
                out = []
                for level in range(LEVELS):
                    dot = dot + dots[level, at, :]
                    key = widen(wide[level, at, :], CHUNK // LANES)
                    grow = jnp.exp2(dot * key * row[level : level + 1, :])
                    out.append(acc[level] + fold(grow))
                return tuple(out)

            start = tuple(jnp.zeros((8, CHUNK), F32) for _ in range(LEVELS))
            acc = lax.fori_loop(0, KEYS // STEP_F, body, start)
            rows = [jnp.sum(a, axis=0, keepdims=True) for a in acc]
            found = jnp.concatenate(rows + [jnp.ones((2, CHUNK), F32)], axis=0)
            sums[8 * side : 8 * side + 8, part * CHUNK : (part + 1) * CHUNK] = found
        sums[8 * side : 8 * side + 8, :ROWS] = sums[8 * side : 8 * side + 8, :ROWS] + grown
    total = jnp.sum(matched[...], axis=1, keepdims=True)
    sums[16:24, :] = jnp.broadcast_to(total, (8, QUERIES))


def suffix(rows):
    out = [rows[LEVELS - 1 : LEVELS]]
    for level in range(LEVELS - 2, -1, -1):
        out.append(out[-1] + rows[level : level + 1])
    return jnp.concatenate(out[::-1] + [jnp.zeros((2, rows.shape[1]), F32)], axis=0)


def columns_of(rows):
    n = rows.shape[1]
    return jnp.transpose(jnp.concatenate([rows, jnp.zeros((LANES - 8, n), F32)], axis=0))


def by_lane(parts):
    lane = iota(parts[0].shape, 1)
    return jnp.where(lane < EDGES[1], parts[0], jnp.where(lane < EDGES[2], parts[1], parts[2]))


def pick(parts, block):
    if block == 0:
        return by_lane(parts[:3])
    return parts[3 if block == 1 else (4 if block < 4 else 5)]


def loss_tail(loss):
    high = loss.astype(BF).astype(F32)
    mid = (loss - high).astype(BF).astype(F32)
    low = (loss - high) - mid
    lane = iota(loss.shape, 1)
    return jnp.where(lane == 0, high, jnp.where(lane == 1, mid, jnp.where(lane == 2, low, 0.0)))


def backward(xs, xo, rq, ro, matched, keys, kn, s0, s1, s2, s3,
             send, gq0, gown, gother, dots, wide, ws, ea, acc_q):
    parts = (s0, s1, s2, s3)
    total = []
    for block in range(2 * RING):
        flip, s = divmod(block, RING)
        found = None
        for t in range(RING):
            at = flip * CHUNK + ((s - t) % RING) * ROWS
            more = parts[t][:16, at : at + ROWS]
            found = more if found is None else found + more
        total.append(found)
    total = jnp.concatenate(total, axis=1)
    inverse = 1.0 / total
    logs = jnp.log(total)
    all_matched = sum(p[16:24, :LANES] for p in parts)
    each = jnp.sum(logs[:8] + logs[8:], axis=1, keepdims=True)
    tail = loss_tail(jnp.broadcast_to(each, (8, LANES)) - 2.0 * all_matched)
    send[:, 2 * D :] = jnp.concatenate([tail] * (KEYS // 8), axis=0).astype(BF)

    own = matched[...]
    grown = jnp.exp(own)
    m = grown * inverse[:8, :ROWS] + grown * inverse[8:, :ROWS] - 2.0
    cross = columns_of(suffix(SCALE * m * rq[0, :, :ROWS] * rq[1, :, :ROWS]))
    crosses = [spread(cross, level) for level in range(LEVELS)]
    ones = jnp.ones((LANES, LANES), BF)

    for side in range(2):
        base = (1 - side) * D
        norms = kn[side]
        for level in range(LEVELS):
            wide[level] = spread(norms, level)
        for part, (queries, scale) in enumerate(((xs, rq), (xo, ro))):
            raw_scores(keys, queries, dots, side)
            cols = slice(part * CHUNK, (part + 1) * CHUNK)
            row = (SCALE * LOG2E) * scale[side]
            gain = SCALE * scale[side] * inverse[8 * side : 8 * side + 8, cols]

            def body(t, acc):
                at = pl.ds(pl.multiple_of(t * STEP_B, STEP_B), STEP_B)
                dot = jnp.zeros((STEP_B, CHUNK), F32)
                out = []
                for level in range(LEVELS):
                    dot = dot + dots[level, at, :]
                    key = widen(wide[level, at, :], CHUNK // LANES)
                    scaled = dot * key
                    grow = jnp.exp2(scaled * row[level : level + 1, :])
                    weight = grow * gain[level : level + 1, :]
                    ws[level, at, cols] = (weight * key).astype(BF)
                    pa = weight * scaled
                    out.append(acc[level] + fold(pa))
                    summed = pa[:, :LANES]
                    for b in range(1, CHUNK // LANES):
                        summed = summed + pa[:, b * LANES : (b + 1) * LANES]
                    if part == 0:
                        ea[level, at, :] = summed
                    else:
                        ea[level, at, :] = ea[level, at, :] + summed
                return tuple(out)

            start = tuple(jnp.zeros((8, CHUNK), F32) for _ in range(LEVELS))
            acc = lax.fori_loop(0, KEYS // STEP_B, body, start)
            rows = [jnp.sum(a, axis=0, keepdims=True) for a in acc]
            ca = jnp.concatenate(rows + [jnp.zeros((2, CHUNK), F32)], axis=0)
            if part == 0:
                ca = jnp.concatenate([ca[:, :ROWS] + m * own, ca[:, ROWS:]], axis=1)
            ca = columns_of(suffix(ca * scale[side] * scale[side]))
            cas = [spread(ca, level) for level in range(LEVELS)]

            for level in range(LEVELS - 1, -1, -1):
                width = max(EDGES[level + 1], LANES)
                more = dot_tn(ws[level, :, cols], keys[:, base : base + width])
                if level < 2:
                    more = jnp.where(iota((CHUNK, LANES), 1) < EDGES[level + 1], more, 0.0)
                acc_q[:, :width] = more if level == LEVELS - 1 else acc_q[:, :width] + more
            for block in range(D // LANES):
                at = slice(block * LANES, (block + 1) * LANES)
                value = acc_q[:, at] - pick(cas, block) * queries[side, :, at].astype(F32)
                if part == 0:
                    partner = xs[1 - side, :ROWS, at].astype(F32)
                    gq0[side, :, at] = value[:ROWS] + pick(crosses, block) * partner
                    gown[side, :, at] = value[ROWS:].astype(BF)
                else:
                    gother[side, :, at] = value.astype(BF)

        ebs = [None] * LEVELS
        held = None
        for level in range(LEVELS - 1, -1, -1):
            term = sums_down(ea[level], ones) * wide[level] * wide[level]
            held = term if held is None else held + term
            ebs[level] = held
        for lower, upper in ((0, 128), (128, 256), (256, 512), (512, 1024)):
            grad = None
            for level in range(2 if lower == 0 else EDGES.index(lower), LEVELS):
                more = dot_nn(ws[level, :, :CHUNK], xs[side, :, lower:upper])
                more = more + dot_nn(ws[level, :, CHUNK:], xo[side, :, lower:upper])
                grad = more if grad is None else grad + more
            if lower == 0:
                for level in (1, 0):
                    more = dot_nn(ws[level, :, :CHUNK], xs[side, :, lower:upper])
                    more = more + dot_nn(ws[level, :, CHUNK:], xo[side, :, lower:upper])
                    grad = grad + jnp.where(iota((KEYS, LANES), 1) < EDGES[level + 1], more, 0.0)
            for block in range(lower // LANES, upper // LANES):
                rel = slice(block * LANES - lower, (block + 1) * LANES - lower)
                home = slice(base + block * LANES, base + (block + 1) * LANES)
                value = grad[:, rel] - pick(ebs, block) * keys[:, home].astype(F32)
                send[:, home] = value.astype(BF)


def after_core(g0, own, other, kept, x1, x2, x3):
    for side in range(2):
        place = slice(side * ROWS, (side + 1) * ROWS)
        kept[place, :] = g0[side] + other[side, :ROWS, :].astype(F32)
        for s, ref in ((1, x1), (2, x2), (3, x3)):
            mine = own[side, (s - 1) * ROWS : s * ROWS, :].astype(F32)
            theirs = other[side, s * ROWS : (s + 1) * ROWS, :].astype(F32)
            ref[place, :] = (mine + theirs).astype(BF)


def at_end(got, after, image_bank, text_bank, losses):
    for at in range(0, 2 * D, 2 * LANES):
        value = fold(got[:, at : at + 2 * LANES].astype(F32))
        if at < D:
            image_bank[:, at : at + 2 * LANES] = value
        else:
            text_bank[:, at - D : at - D + 2 * LANES] = value
    tail = fold(got[:, 2 * D :].astype(F32)) * (1.0 / 65536.0)
    for level in range(LEVELS):
        losses[level] = jnp.sum(tail[level : level + 1, :])


def query_end(own, r1, r2, r3, grad_image, grad_text):
    for kind, ref in ((0, grad_image), (1, grad_text)):
        rows = slice(kind * ROWS, (kind + 1) * ROWS)
        value = own[rows, :] + r1[rows, :].astype(F32)
        ref[...] = value + (r2[rows, :].astype(F32) + r3[rows, :].astype(F32))


def shaped(shape, dtype=F32):
    return jax.ShapeDtypeStruct(shape, dtype)


def call(kernel, outs, scratch=()):
    return pl.pallas_call(
        kernel,
        out_shape=tuple(outs),
        scratch_shapes=tuple(scratch),
        compiler_params=pltpu.CompilerParams(vmem_limit_bytes=VMEM_LIMIT),
    )


def move(value, step, flip=0):
    pairs = []
    for i in range(2 * RING):
        x, c = divmod(i, 2)
        pairs.append((i, 2 * ((x + step) % RING) + (c ^ flip)))
    return lax.ppermute(value, ("x", "c"), pairs)


def exchange(value):
    return lax.all_to_all(value, ("y", "z"), 0, 0, tiled=True)


def prepare_call(queries, late):
    return pl.pallas_call(
        prepare,
        out_shape=(shaped((2, CHUNK, D), BF), shaped((2, 8, CHUNK)), shaped((8, ROWS))),
        in_specs=[pl.BlockSpec(memory_space=pltpu.VMEM)] * 4 + [pl.BlockSpec(memory_space=pl.ANY)],
        compiler_params=pltpu.CompilerParams(vmem_limit_bytes=VMEM_LIMIT),
    )(*queries, late)


def forward_call(*values):
    return call(
        forward,
        [shaped((24, QUERIES)), shaped((2, KEYS, LANES))],
        [pltpu.VMEM((LEVELS, KEYS, CHUNK), F32), pltpu.VMEM((LEVELS, KEYS, LANES), F32)],
    )(*values)


def backward_call(*values):
    return call(
        backward,
        [
            shaped((KEYS, 2 * D + LANES), BF),
            shaped((2, ROWS, D)),
            shaped((2, CHUNK - ROWS, D), BF),
            shaped((2, CHUNK, D), BF),
        ],
        [
            pltpu.VMEM((LEVELS, KEYS, CHUNK), F32),
            pltpu.VMEM((LEVELS, KEYS, LANES), F32),
            pltpu.VMEM((LEVELS, KEYS, QUERIES), BF),
            pltpu.VMEM((LEVELS, KEYS, LANES), F32),
            pltpu.VMEM((CHUNK, D), F32),
        ],
    )(*values)


def on_device(image, text, image_bank, text_bank):
    query = jnp.concatenate([image, text], axis=0)
    queries = [query] + [move(query, s) for s in (1, 2, 3)]
    bank = jnp.concatenate([image_bank, text_bank], axis=1)
    keys = exchange(jnp.tile(bank, (PAIRS, 1)))
    xs, rq, matched = prepare_call(queries, keys)
    xo, ro = move(xs, 0, 1), move(rq, 0, 1)

    sums, kn = forward_call(xs, xo, rq, ro, matched, keys)
    theirs = move(sums, 0, 1)
    sums = sums + jnp.concatenate([theirs[:, CHUNK:], theirs[:, :CHUNK]], axis=1)
    found = [sums] + [move(sums, s) for s in (1, 2, 3)]
    send, gq0, gown, gother = backward_call(xs, xo, rq, ro, matched, keys, kn, *found)

    got = exchange(send)
    kept, x1, x2, x3 = call(after_core, [shaped((2 * ROWS, D))] + [shaped((2 * ROWS, D), BF)] * 3)(
        gq0, gown, move(gother, 0, 1)
    )
    back = [move(g, -s) for s, g in ((1, x1), (2, x2), (3, x3))]
    grad_image, grad_text = call(query_end, [shaped((ROWS, D))] * 2)(kept, *back)
    grad_image_bank, grad_text_bank, losses = pl.pallas_call(
        at_end,
        out_shape=(shaped((8, D)), shaped((8, D)), shaped((LEVELS,))),
        in_specs=[pl.BlockSpec(memory_space=pltpu.VMEM), pl.BlockSpec(memory_space=pl.ANY)],
        out_specs=(pl.BlockSpec(memory_space=pltpu.VMEM),) * 2 + (pl.BlockSpec(memory_space=pltpu.SMEM),),
        compiler_params=pltpu.CompilerParams(vmem_limit_bytes=VMEM_LIMIT),
    )(got, grad_image)
    return losses, grad_image, grad_text, grad_image_bank, grad_text_bank


def solution(mesh):
    torus = Mesh(mesh.devices.reshape(4, 8, 4, 2), ("y", "z", "x", "c"))
    rows = P(("y", "z", "x", "c"), None)
    return jax.shard_map(
        on_device,
        mesh=torus,
        in_specs=(rows,) * 4,
        out_specs=(P(),) + (rows,) * 4,
        check_vma=False,
    )
```

```python
import jax
import jax.numpy as jnp
from jax import lax
from jax.experimental import pallas as pl
from jax.experimental.pallas import tpu as pltpu
from jax.sharding import Mesh, PartitionSpec as P

SCALE = 20.0
EPS = 1e-06
LOG2E = 1.4426950408889634
LEVELS = 6
EDGES = (0, 32, 64, 128, 256, 512, 1024)
D = 1024
ROWS = 128
RING = 4
CHUNK = ROWS * RING
KEYS = 256
BANK = 2 * KEYS
LANES = 128
PAIRS = 8
NEAR = 64
STEP_F = 32
STEP_B = 32
VMEM_LIMIT = 56 * 1024 * 1024
BF = jnp.bfloat16
F32 = jnp.float32


def dot_nt(left, right):
    return lax.dot_general(left, right, (((1,), (1,)), ((), ())), preferred_element_type=F32)


def dot_nn(left, right):
    return lax.dot_general(left, right, (((1,), (0,)), ((), ())), preferred_element_type=F32)


def dot_tn(left, right):
    return lax.dot_general(left, right, (((0,), (0,)), ((), ())), preferred_element_type=F32)


def iota(shape, axis):
    return lax.broadcasted_iota(jnp.int32, shape, axis)


def level_mask(shape, level_axis):
    width = jnp.left_shift(32, jnp.minimum(iota(shape, level_axis), LEVELS - 1))
    return jnp.where(iota(shape, 1 - level_axis) < width, 1.0, 0.0).astype(BF)


def halves(values):
    high = values.astype(BF)
    return high, (values - high.astype(F32)).astype(BF)


def sums_across(values, mask):
    high, low = halves(values)
    return dot_nt(mask, high) + dot_nt(mask, low)


def sums_down(values, mask):
    high, low = halves(values)
    return dot_nn(high, mask) + dot_nn(low, mask)


def pick_lanes(values, level):
    lane = iota(values.shape, 1)
    keep = (lane >= EDGES[level]) & (lane < EDGES[level + 1])
    return jnp.where(keep, values.astype(F32), 0.0).astype(BF)


def keys_of(keys, side):
    return slice((1 - side) * D, (2 - side) * D)


def raw_scores(keys, queries, dots, side):
    base = (1 - side) * D
    for level in range(3):
        dots[level] = dot_nt(keys[:, base : base + LANES], pick_lanes(queries[side, :, :LANES], level))
    for level in range(3, LEVELS):
        lower, upper = EDGES[level], EDGES[level + 1]
        dots[level] = dot_nt(keys[:, base + lower : base + upper], queries[side, :, lower:upper])


def fold(values):
    return jnp.sum(values.reshape(values.shape[0] // 8, 8, values.shape[1]), axis=0)


def widen(values, n):
    return jnp.concatenate([values] * n, axis=1)


def spread(cols, level):
    return jnp.broadcast_to(cols[:, level : level + 1], (cols.shape[0], LANES))


def prepare(q0, q1, q2, q3, rq, matched):
    across = level_mask((16, D), 0)
    for side in range(2):
        rows = slice(side * ROWS, (side + 1) * ROWS)
        for s, block in enumerate((q0[rows, :], q1[rows, :], q2[rows, :], q3[rows, :])):
            wide = block.astype(F32)
            found = lax.rsqrt(sums_across(wide * wide, across) + EPS)
            rq[side, :, s * ROWS : (s + 1) * ROWS] = found[:8]
    product = q0[:ROWS, :].astype(F32) * q0[ROWS:, :].astype(F32)
    matched[...] = SCALE * sums_across(product, across)[:8] * rq[0, :, :ROWS] * rq[1, :, :ROWS]


def prepare_keys(b0, b1, b2, b3, after, kn):
    down = level_mask((D, LANES), 1)
    for s, block in enumerate((b0, b1, b2, b3)):
        for side in range(2):
            y = block[:, keys_of(block, side)].astype(F32)
            kn[side, s * NEAR : (s + 1) * NEAR, :] = lax.rsqrt(sums_down(y * y, down) + EPS)


def fetch(blocks, xs, ks, sems):
    q0, q1, q2, q3 = blocks[:4]
    count = 0

    def start(source, target):
        nonlocal count
        copy = pltpu.make_async_copy(source, target, sems.at[count])
        copy.start()
        count += 1
        return copy

    def queries(side):
        rows = slice(side * ROWS, (side + 1) * ROWS)
        parts = (q0.at[rows, :], q1.at[rows, :], q2.at[rows, :], q3.at[rows, :])
        return [start(p, xs.at[side, s * ROWS : (s + 1) * ROWS, :]) for s, p in enumerate(parts)]

    def keys(part):
        found = blocks[4 + 4 * part : 8 + 4 * part]
        return [start(b, ks.at[part * KEYS + s * NEAR : part * KEYS + (s + 1) * NEAR, :]) for s, b in enumerate(found)]

    first = queries(0)
    return [first, keys(0), keys(1), queries(1)]


def arrive(copies):
    for copy in copies:
        copy.wait()


def forward(*refs):
    rq, matched, n0, n1 = refs[12:16]
    sums, xs, ks, dots, wide, sems = refs[16:]
    near_queries, near_keys, far_keys, other_queries = fetch(refs[:12], xs, ks, sems)
    grown = jnp.exp(matched[...])
    total = jnp.broadcast_to(jnp.sum(matched[...], axis=1, keepdims=True), (8, ROWS))
    spare = [jnp.concatenate([total[r : r + 1] for r in rows], axis=1) for rows in ((0, 1, 2, 3), (4, 5, 5, 5))]
    for side in range(2):
        row = (SCALE * LOG2E) * rq[side]
        arrive(near_queries if side == 0 else other_queries)
        acc = tuple(jnp.zeros((8, CHUNK), F32) for _ in range(LEVELS))
        for part, norms in enumerate((n0, n1)):
            if side == 0:
                arrive((near_keys, far_keys)[part])
            rows = slice(part * KEYS, (part + 1) * KEYS)
            for level in range(LEVELS):
                wide[level, rows, :] = spread(norms[side], level)
            raw_scores(ks.at[rows, :], xs, dots.at[part], side)

            def body(t, acc):
                at = pl.ds(pl.multiple_of(t * STEP_F, STEP_F), STEP_F)
                to = pl.ds(pl.multiple_of(part * KEYS + t * STEP_F, STEP_F), STEP_F)
                dot = jnp.zeros((STEP_F, CHUNK), F32)
                out = []
                for level in range(LEVELS):
                    dot = dot + dots[part, level, at, :]
                    key = widen(wide[level, to, :], CHUNK // LANES)
                    grow = jnp.exp2(dot * key * row[level : level + 1, :])
                    out.append(acc[level] + fold(grow))
                return tuple(out)

            acc = lax.fori_loop(0, KEYS // STEP_F, body, acc, unroll=True)
        rows = [jnp.sum(a, axis=0, keepdims=True) for a in acc]
        sums[8 * side : 8 * side + 8, :] = jnp.concatenate(rows + spare, axis=0)
        sums[8 * side : 8 * side + LEVELS, :ROWS] = sums[8 * side : 8 * side + LEVELS, :ROWS] + grown[:LEVELS]


def suffix(rows):
    out = [rows[LEVELS - 1 : LEVELS]]
    for level in range(LEVELS - 2, -1, -1):
        out.append(out[-1] + rows[level : level + 1])
    return jnp.concatenate(out[::-1] + [jnp.zeros((2, rows.shape[1]), F32)], axis=0)


def columns_of(rows):
    n = rows.shape[1]
    return jnp.transpose(jnp.concatenate([rows, jnp.zeros((LANES - 8, n), F32)], axis=0))


def by_lane(parts):
    lane = iota(parts[0].shape, 1)
    return jnp.where(lane < EDGES[1], parts[0], jnp.where(lane < EDGES[2], parts[1], parts[2]))


def pick(parts, block):
    if block == 0:
        return by_lane(parts[:3])
    return parts[3 if block == 1 else (4 if block < 4 else 5)]


def put_loss(ref, loss):
    ref[:, 2 * D :] = jnp.concatenate([loss_tail(loss)] * (NEAR // 8), axis=0).astype(ref.dtype)


def loss_of(ref):
    tail = ref[:, 2 * D :].astype(F32)[:8]
    return jnp.broadcast_to(jnp.sum(tail, axis=1, keepdims=True), (8, LANES))


def loss_tail(loss):
    high = loss.astype(BF).astype(F32)
    mid = (loss - high).astype(BF).astype(F32)
    low = (loss - high) - mid
    lane = iota(loss.shape, 1)
    return jnp.where(lane == 0, high, jnp.where(lane == 1, mid, jnp.where(lane == 2, low, 0.0)))


def backward(*refs):
    rq, matched, n0, n1, s0, s1, s2, s3 = refs[12:20]
    outs, loss = refs[20:26], refs[26]
    xs, ks, gq0, gq1, gq2, gq3, gown, gother, dots, wide, ws, ea, acc_q, sems, out_sems = refs[27:]
    near_queries, near_keys, far_keys, other_queries = fetch(refs[:12], xs, ks, sems)
    leaving = []

    def leave(n, rows, cols):
        source = (gq0, gq1, gq2, gq3, gown, gother)[n]
        copy = pltpu.make_async_copy(source.at[rows, cols], outs[n].at[rows, cols], out_sems.at[len(leaving)])
        copy.start()
        leaving.append(copy)

    parts = (s0, s1, s2, s3)
    total = []
    for s in range(RING):
        found = None
        for t in range(RING):
            at = ((s - t) % RING) * ROWS
            more = parts[t][:, at : at + ROWS]
            found = more if found is None else found + more
        total.append(found)
    total = jnp.concatenate(total, axis=1)
    inverse = 1.0 / total
    logs = jnp.log(total)
    spare = (s0[6:8, :] + s1[6:8, :]) + (s2[6:8, :] + s3[6:8, :])
    all_matched = [spare[r // 4 : r // 4 + 1, (r % 4) * ROWS : (r % 4 + 1) * ROWS] for r in range(LEVELS)]
    all_matched = jnp.concatenate(all_matched + [jnp.zeros((2, ROWS), F32)], axis=0)
    each = jnp.sum(logs[:8] + logs[8:], axis=1, keepdims=True)
    mine = jnp.broadcast_to(each, (8, LANES)) - 2.0 * all_matched
    loss[...] = mine
    gother[KEYS:, :LANES] = jnp.concatenate([loss_tail(mine)] * 2, axis=0).astype(BF)
    gother[KEYS:, LANES:] = jnp.zeros((16, 2 * D - LANES), BF)

    own = matched[...]
    grown = jnp.exp(own)
    m = grown * inverse[:8, :ROWS] + grown * inverse[8:, :ROWS] - 2.0
    cross = columns_of(suffix(SCALE * m * rq[0, :, :ROWS] * rq[1, :, :ROWS]))
    crosses = [spread(cross, level) for level in range(LEVELS)]
    ones = jnp.ones((LANES, LANES), BF)

    for side in range(2):
        base = (1 - side) * D
        if side == 0:
            arrive(near_queries)
        row = (SCALE * LOG2E) * rq[side]
        gain = SCALE * rq[side] * inverse[8 * side : 8 * side + 8, :]
        acc = tuple(jnp.zeros((8, CHUNK), F32) for _ in range(LEVELS))
        for part, norms in enumerate((n0, n1)):
            if side == 0:
                arrive((near_keys, far_keys)[part])
            rows = slice(part * KEYS, (part + 1) * KEYS)
            for level in range(LEVELS):
                wide[level, rows, :] = spread(norms[side], level)
            raw_scores(ks.at[rows, :], xs, dots.at[part], side)

            def body(t, acc):
                at = pl.ds(pl.multiple_of(t * STEP_B, STEP_B), STEP_B)
                to = pl.ds(pl.multiple_of(part * KEYS + t * STEP_B, STEP_B), STEP_B)
                dot = jnp.zeros((STEP_B, CHUNK), F32)
                sums = []
                for level in range(LEVELS):
                    dot = dot + dots[part, level, at, :]
                    key = widen(wide[level, to, :], CHUNK // LANES)
                    scaled = dot * key
                    grow = jnp.exp2(scaled * row[level : level + 1, :])
                    weight = grow * gain[level : level + 1, :]
                    ws[level, to, :] = (weight * key).astype(BF)
                    pa = weight * scaled
                    sums.append(acc[level] + fold(pa))
                    summed = pa[:, :LANES]
                    for b in range(1, CHUNK // LANES):
                        summed = summed + pa[:, b * LANES : (b + 1) * LANES]
                    ea[level, to, :] = summed
                return tuple(sums)

            acc = lax.fori_loop(0, KEYS // STEP_B, body, acc, unroll=True)

        ebs = [None] * LEVELS
        held = None
        for level in range(LEVELS - 1, -1, -1):
            term = sums_down(ea[level], ones) * wide[level] * wide[level]
            held = term if held is None else held + term
            ebs[level] = held
        for lower, upper in ((0, 128), (128, 256), (256, 512), (512, 1024)):
            grad = None
            for level in range(2 if lower == 0 else EDGES.index(lower), LEVELS):
                more = dot_nn(ws[level], xs[side, :, lower:upper])
                grad = more if grad is None else grad + more
            if lower == 0:
                for level in (1, 0):
                    more = dot_nn(ws[level], xs[side, :, lower:upper])
                    grad = grad + jnp.where(iota((BANK, LANES), 1) < EDGES[level + 1], more, 0.0)
            for block in range(lower // LANES, upper // LANES):
                rel = slice(block * LANES - lower, (block + 1) * LANES - lower)
                home = slice(base + block * LANES, base + (block + 1) * LANES)
                value = grad[:, rel] - pick(ebs, block) * ks[:, home].astype(F32)
                gown[:, home] = value[:KEYS]
                gother[:KEYS, home] = value[KEYS:].astype(BF)
        leave(4, slice(0, KEYS), slice(base, base + D))
        leave(5, slice(0, KEYS + 16), slice(base, base + D))

        rows = [jnp.sum(a, axis=0, keepdims=True) for a in acc]
        if side == 0:
            arrive(other_queries)
        ca = jnp.concatenate(rows + [jnp.zeros((2, CHUNK), F32)], axis=0)
        ca = jnp.concatenate([ca[:, :ROWS] + m * own, ca[:, ROWS:]], axis=1)
        ca = columns_of(suffix(ca * rq[side] * rq[side]))
        cas = [spread(ca, level) for level in range(LEVELS)]
        for level in range(LEVELS - 1, -1, -1):
            width = max(EDGES[level + 1], LANES)
            more = dot_tn(ws[level], ks[:, base : base + width])
            if level < 2:
                more = jnp.where(iota((CHUNK, LANES), 1) < EDGES[level + 1], more, 0.0)
            acc_q[:, :width] = more if level == LEVELS - 1 else acc_q[:, :width] + more
        place = slice(side * ROWS, (side + 1) * ROWS)
        for block in range(D // LANES):
            at = slice(block * LANES, (block + 1) * LANES)
            value = acc_q[:, at] - pick(cas, block) * xs[side, :, at].astype(F32)
            partner = xs[1 - side, :ROWS, at].astype(F32)
            gq0[place, at] = value[:ROWS] + pick(crosses, block) * partner
            for s, ref in ((1, gq1), (2, gq2), (3, gq3)):
                ref[place, at] = value[s * ROWS : (s + 1) * ROWS].astype(BF)
        for n in range(RING):
            leave(n, place, slice(0, D))
    arrive(leaving)


def after_core(own, other, loss, kept, y1, y2, y3):
    tail = other[KEYS:, :LANES].astype(F32)[:8]
    total = loss[...] + jnp.broadcast_to(jnp.sum(tail, axis=1, keepdims=True), (8, LANES))
    for s, ref in enumerate((kept, y1, y2, y3)):
        rows = slice(s * NEAR, (s + 1) * NEAR)
        ref[:, : 2 * D] = (own[rows, :] + other[rows, :].astype(F32)).astype(ref.dtype)
        put_loss(ref, total)


def after_y(own, r1, r2, r3, *rest):
    send = rest[-1]
    for at in range(0, 2 * D, LANES):
        cols = slice(at, at + LANES)
        value = own[:, cols] + r1[:, cols].astype(F32)
        send[:, cols] = (value + (r2[:, cols].astype(F32) + r3[:, cols].astype(F32))).astype(BF)
    put_loss(send, (loss_of(own) + loss_of(r1)) + (loss_of(r2) + loss_of(r3)))


def at_end(got, after, image_bank, text_bank, losses):
    for at in range(0, 2 * D, 2 * LANES):
        value = fold(got[:, at : at + 2 * LANES].astype(F32))
        if at < D:
            image_bank[:, at : at + 2 * LANES] = value
        else:
            text_bank[:, at - D : at - D + 2 * LANES] = value
    tail = fold(got[:, 2 * D :].astype(F32)) * (1.0 / 65536.0)
    for level in range(LEVELS):
        losses[level] = jnp.sum(tail[level : level + 1, :])


def query_end(own, r1, r2, r3, grad_image, grad_text):
    for kind, ref in ((0, grad_image), (1, grad_text)):
        rows = slice(kind * ROWS, (kind + 1) * ROWS)
        value = own[rows, :] + r1[rows, :].astype(F32)
        ref[...] = value + (r2[rows, :].astype(F32) + r3[rows, :].astype(F32))


def shaped(shape, dtype=F32):
    return jax.ShapeDtypeStruct(shape, dtype)


def call(kernel, outs, scratch=()):
    return pl.pallas_call(
        kernel,
        out_shape=tuple(outs),
        scratch_shapes=tuple(scratch),
        compiler_params=pltpu.CompilerParams(vmem_limit_bytes=VMEM_LIMIT),
    )


def move(value, step, flip=0):
    pairs = []
    for i in range(2 * RING):
        x, c = divmod(i, 2)
        pairs.append((i, 2 * ((x + step) % RING) + (c ^ flip)))
    return lax.ppermute(value, ("x", "c"), pairs)


def along_y(value, step):
    n = lax.axis_size("y")
    return lax.ppermute(value, "y", [(i, (i + step) % n) for i in range(n)])


def exchange(value):
    return lax.all_to_all(value, "z", 0, 0, tiled=True)


ANYWHERE = pl.BlockSpec(memory_space=pl.ANY)
INSIDE = pl.BlockSpec(memory_space=pltpu.VMEM)


def placed(kernel, ins, outs, shapes, scratch=()):
    return pl.pallas_call(
        kernel,
        out_shape=tuple(shapes),
        in_specs=list(ins),
        out_specs=tuple(outs),
        scratch_shapes=tuple(scratch),
        compiler_params=pltpu.CompilerParams(vmem_limit_bytes=VMEM_LIMIT),
    )


def on_device(image, text, image_bank, text_bank):
    query = jnp.concatenate([image, text], axis=0)
    queries = [query] + [move(query, s) for s in (1, 2, 3)]
    bank = jnp.concatenate([image_bank, text_bank], axis=1)
    near = exchange(jnp.tile(bank, (PAIRS, 1)))
    around = [near] + [along_y(near, s) for s in (1, 2, 3)]
    rq, matched = call(prepare, [shaped((2, 8, CHUNK)), shaped((8, ROWS))])(*queries)
    (n0,) = placed(prepare_keys, [INSIDE] * 4 + [ANYWHERE], [INSIDE], [shaped((2, KEYS, LANES))])(*around, matched)
    n1 = move(n0, 0, 1)
    far = [move(b, 0, 1) for b in around]
    blocks = queries + around + far
    held = [
        pltpu.VMEM((2, CHUNK, D), BF),
        pltpu.VMEM((BANK, 2 * D), BF),
    ]
    scores = [pltpu.VMEM((2, LEVELS, KEYS, CHUNK), F32), pltpu.VMEM((LEVELS, BANK, LANES), F32)]

    (sums,) = placed(
        forward,
        [ANYWHERE] * 12 + [INSIDE] * 4,
        [INSIDE],
        [shaped((16, CHUNK))],
        held + scores + [pltpu.SemaphoreType.DMA((16,))],
    )(*blocks, rq, matched, n0, n1)
    found = [sums] + [move(sums, s) for s in (1, 2, 3)]
    grads = [
        shaped((2 * ROWS, D)),
        shaped((2 * ROWS, D), BF),
        shaped((2 * ROWS, D), BF),
        shaped((2 * ROWS, D), BF),
        shaped((KEYS, 2 * D)),
        shaped((KEYS + 16, 2 * D), BF),
    ]
    gq0, gq1, gq2, gq3, gown, gother, loss = placed(
        backward,
        [ANYWHERE] * 12 + [INSIDE] * 8,
        [ANYWHERE] * 6 + [INSIDE],
        grads + [shaped((8, LANES))],
        held
        + [pltpu.VMEM(g.shape, g.dtype) for g in grads]
        + scores
        + [
            pltpu.VMEM((LEVELS, BANK, CHUNK), BF),
            pltpu.VMEM((LEVELS, BANK, LANES), F32),
            pltpu.VMEM((CHUNK, D), F32),
            pltpu.SemaphoreType.DMA((16,)),
            pltpu.SemaphoreType.DMA((12,)),
        ],
    )(*blocks, rq, matched, n0, n1, *found)

    back = [move(g, -s) for s, g in ((1, gq1), (2, gq2), (3, gq3))]
    kept, y1, y2, y3 = call(
        after_core,
        [shaped((NEAR, 2 * D + LANES))] + [shaped((NEAR, 2 * D + LANES), BF)] * 3,
    )(gown, move(gother, 0, 1), loss)
    summed = [along_y(g, -s) for s, g in ((1, y1), (2, y2), (3, y3))]
    (send,) = placed(
        after_y, [INSIDE] * 4 + [ANYWHERE] * 1, [INSIDE], [shaped((NEAR, 2 * D + LANES), BF)]
    )(kept, *summed, back[0])
    got = exchange(send)
    grad_image, grad_text = call(query_end, [shaped((ROWS, D))] * 2)(gq0, *back)
    grad_image_bank, grad_text_bank, losses = placed(
        at_end,
        [INSIDE, ANYWHERE],
        [INSIDE, INSIDE, pl.BlockSpec(memory_space=pltpu.SMEM)],
        [shaped((8, D)), shaped((8, D)), shaped((LEVELS,))],
    )(got, grad_image)
    return losses, grad_image, grad_text, grad_image_bank, grad_text_bank


def solution(mesh):
    torus = Mesh(mesh.devices.reshape(4, 8, 4, 2), ("y", "z", "x", "c"))
    rows = P(("y", "z", "x", "c"), None)
    return jax.shard_map(
        on_device,
        mesh=torus,
        in_specs=(rows,) * 4,
        out_specs=(P(),) + (rows,) * 4,
        check_vma=False,
    )
```

```python
import jax
import jax.numpy as jnp
from jax import lax
from jax.experimental import pallas as pl
from jax.experimental.pallas import tpu as pltpu
from jax.sharding import Mesh, PartitionSpec as P

SCALE = 20.0
EPS = 1e-06
LOG2E = 1.4426950408889634
LEVELS = 6
EDGES = (0, 32, 64, 128, 256, 512, 1024)
D = 1024
ROWS = 128
RING = 4
CHUNK = ROWS * RING
KEYS = 256
BANK = 2 * KEYS
LANES = 128
PAIRS = 8
NEAR = 64
STEP_F = 32
STEP_B = 32
VMEM_LIMIT = 56 * 1024 * 1024
BF = jnp.bfloat16
F32 = jnp.float32


def dot_nt(left, right):
    return lax.dot_general(left, right, (((1,), (1,)), ((), ())), preferred_element_type=F32)


def dot_nn(left, right):
    return lax.dot_general(left, right, (((1,), (0,)), ((), ())), preferred_element_type=F32)


def dot_tn(left, right):
    return lax.dot_general(left, right, (((0,), (0,)), ((), ())), preferred_element_type=F32)


def iota(shape, axis):
    return lax.broadcasted_iota(jnp.int32, shape, axis)


def level_mask(shape, level_axis):
    width = jnp.left_shift(32, jnp.minimum(iota(shape, level_axis), LEVELS - 1))
    return jnp.where(iota(shape, 1 - level_axis) < width, 1.0, 0.0).astype(BF)


def halves(values):
    high = values.astype(BF)
    return high, (values - high.astype(F32)).astype(BF)


def sums_across(values, mask):
    high, low = halves(values)
    return dot_nt(mask, high) + dot_nt(mask, low)


def sums_down(values, mask):
    high, low = halves(values)
    return dot_nn(high, mask) + dot_nn(low, mask)


def pick_lanes(values, level):
    lane = iota(values.shape, 1)
    keep = (lane >= EDGES[level]) & (lane < EDGES[level + 1])
    return jnp.where(keep, values.astype(F32), 0.0).astype(BF)


def keys_of(keys, side):
    return slice((1 - side) * D, (2 - side) * D)


def raw_scores(keys, queries, dots, side):
    base = (1 - side) * D
    for level in range(3):
        dots[level] = dot_nt(keys[:, base : base + LANES], pick_lanes(queries[side, :, :LANES], level))
    for level in range(3, LEVELS):
        lower, upper = EDGES[level], EDGES[level + 1]
        dots[level] = dot_nt(keys[:, base + lower : base + upper], queries[side, :, lower:upper])


def fold(values):
    return jnp.sum(values.reshape(values.shape[0] // 8, 8, values.shape[1]), axis=0)


def widen(values, n):
    return jnp.concatenate([values] * n, axis=1)


def spread(cols, level):
    return jnp.broadcast_to(cols[:, level : level + 1], (cols.shape[0], LANES))


def prepare(q0, q1, q2a, q2b, q3, rq, matched):
    across = level_mask((16, D), 0)
    for side in range(2):
        rows = slice(side * ROWS, (side + 1) * ROWS)
        for s, block in enumerate((q0[rows, :], q1[rows, :], (q2a, q2b)[side][...], q3[rows, :])):
            wide = block.astype(F32)
            found = lax.rsqrt(sums_across(wide * wide, across) + EPS)
            rq[side, :, s * ROWS : (s + 1) * ROWS] = found[:8]
    product = q0[:ROWS, :].astype(F32) * q0[ROWS:, :].astype(F32)
    matched[...] = SCALE * sums_across(product, across)[:8] * rq[0, :, :ROWS] * rq[1, :, :ROWS]


def prepare_keys(b0, b1, b2, b3, after, kn):
    down = level_mask((D, LANES), 1)
    for s, block in enumerate((b0, b1, b2, b3)):
        for side in range(2):
            y = block[:, keys_of(block, side)].astype(F32)
            kn[side, s * NEAR : (s + 1) * NEAR, :] = lax.rsqrt(sums_down(y * y, down) + EPS)


def fetch(blocks, xs, ks, sems):
    q0, q1, q2a, q2b, q3 = blocks[:5]
    count = 0

    def start(source, target):
        nonlocal count
        copy = pltpu.make_async_copy(source, target, sems.at[count])
        copy.start()
        count += 1
        return copy

    def queries(side):
        rows = slice(side * ROWS, (side + 1) * ROWS)
        parts = (q0.at[rows, :], q1.at[rows, :], (q2a, q2b)[side], q3.at[rows, :])
        return [start(p, xs.at[side, s * ROWS : (s + 1) * ROWS, :]) for s, p in enumerate(parts)]

    def keys(part):
        found = blocks[5 + 4 * part : 9 + 4 * part]
        return [start(b, ks.at[part * KEYS + s * NEAR : part * KEYS + (s + 1) * NEAR, :]) for s, b in enumerate(found)]

    first = queries(0)
    return [first, keys(0), keys(1), queries(1)]


def arrive(copies):
    for copy in copies:
        copy.wait()


def forward(*refs):
    rq, matched, n0, n1 = refs[13:17]
    sums, xs, ks, dots, wide, sems = refs[17:]
    near_queries, near_keys, far_keys, other_queries = fetch(refs[:13], xs, ks, sems)
    grown = jnp.exp(matched[...])
    total = jnp.broadcast_to(jnp.sum(matched[...], axis=1, keepdims=True), (8, ROWS))
    spare = [jnp.concatenate([total[r : r + 1] for r in rows], axis=1) for rows in ((0, 1, 2, 3), (4, 5, 5, 5))]
    for side in range(2):
        row = (SCALE * LOG2E) * rq[side]
        arrive(near_queries if side == 0 else other_queries)
        acc = tuple(jnp.zeros((8, CHUNK), F32) for _ in range(LEVELS))
        for part, norms in enumerate((n0, n1)):
            if side == 0:
                arrive((near_keys, far_keys)[part])
            rows = slice(part * KEYS, (part + 1) * KEYS)
            for level in range(LEVELS):
                wide[level, rows, :] = spread(norms[side], level)
            raw_scores(ks.at[rows, :], xs, dots.at[part], side)

            def body(t, acc):
                at = pl.ds(pl.multiple_of(t * STEP_F, STEP_F), STEP_F)
                to = pl.ds(pl.multiple_of(part * KEYS + t * STEP_F, STEP_F), STEP_F)
                dot = jnp.zeros((STEP_F, CHUNK), F32)
                out = []
                for level in range(LEVELS):
                    dot = dot + dots[part, level, at, :]
                    key = widen(wide[level, to, :], CHUNK // LANES)
                    grow = jnp.exp2(dot * key * row[level : level + 1, :])
                    out.append(acc[level] + fold(grow))
                return tuple(out)

            acc = lax.fori_loop(0, KEYS // STEP_F, body, acc, unroll=True)
        rows = [jnp.sum(a, axis=0, keepdims=True) for a in acc]
        sums[8 * side : 8 * side + 8, :] = jnp.concatenate(rows + spare, axis=0)
        sums[8 * side : 8 * side + LEVELS, :ROWS] = sums[8 * side : 8 * side + LEVELS, :ROWS] + grown[:LEVELS]


def suffix(rows):
    out = [rows[LEVELS - 1 : LEVELS]]
    for level in range(LEVELS - 2, -1, -1):
        out.append(out[-1] + rows[level : level + 1])
    return jnp.concatenate(out[::-1] + [jnp.zeros((2, rows.shape[1]), F32)], axis=0)


def columns_of(rows):
    n = rows.shape[1]
    return jnp.transpose(jnp.concatenate([rows, jnp.zeros((LANES - 8, n), F32)], axis=0))


def by_lane(parts):
    lane = iota(parts[0].shape, 1)
    return jnp.where(lane < EDGES[1], parts[0], jnp.where(lane < EDGES[2], parts[1], parts[2]))


def pick(parts, block):
    if block == 0:
        return by_lane(parts[:3])
    return parts[3 if block == 1 else (4 if block < 4 else 5)]


def put_loss(ref, loss):
    ref[:, 2 * D :] = jnp.concatenate([loss_tail(loss)] * (NEAR // 8), axis=0).astype(ref.dtype)


def loss_of(ref):
    tail = ref[:, 2 * D :].astype(F32)[:8]
    return jnp.broadcast_to(jnp.sum(tail, axis=1, keepdims=True), (8, LANES))


def loss_tail(loss):
    high = loss.astype(BF).astype(F32)
    mid = (loss - high).astype(BF).astype(F32)
    low = (loss - high) - mid
    lane = iota(loss.shape, 1)
    return jnp.where(lane == 0, high, jnp.where(lane == 1, mid, jnp.where(lane == 2, low, 0.0)))


def backward(*refs):
    rq, matched, n0, n1, s0, s1, s2, s3 = refs[13:21]
    outs, loss = refs[21:27], refs[27]
    xs, ks, gq0, gq1, gq2, gq3, gown, gother, dots, wide, ws, ea, acc_q, sems, out_sems = refs[28:]
    near_queries, near_keys, far_keys, other_queries = fetch(refs[:13], xs, ks, sems)
    leaving = []

    def leave(n, rows, cols):
        source = (gq0, gq1, gq2, gq3, gown, gother)[n]
        copy = pltpu.make_async_copy(source.at[rows, cols], outs[n].at[rows, cols], out_sems.at[len(leaving)])
        copy.start()
        leaving.append(copy)

    parts = (s0, s1, s2, s3)
    total = []
    for s in range(RING):
        found = None
        for t in range(RING):
            at = ((s - t) % RING) * ROWS
            more = parts[t][:, at : at + ROWS]
            found = more if found is None else found + more
        total.append(found)
    total = jnp.concatenate(total, axis=1)
    inverse = 1.0 / total
    logs = jnp.log(total)
    spare = (s0[6:8, :] + s1[6:8, :]) + (s2[6:8, :] + s3[6:8, :])
    all_matched = [spare[r // 4 : r // 4 + 1, (r % 4) * ROWS : (r % 4 + 1) * ROWS] for r in range(LEVELS)]
    all_matched = jnp.concatenate(all_matched + [jnp.zeros((2, ROWS), F32)], axis=0)
    each = jnp.sum(logs[:8] + logs[8:], axis=1, keepdims=True)
    mine = jnp.broadcast_to(each, (8, LANES)) - 2.0 * all_matched
    loss[...] = mine
    gother[KEYS:, :LANES] = jnp.concatenate([loss_tail(mine)] * 2, axis=0).astype(BF)
    gother[KEYS:, LANES:] = jnp.zeros((16, 2 * D - LANES), BF)

    own = matched[...]
    grown = jnp.exp(own)
    m = grown * inverse[:8, :ROWS] + grown * inverse[8:, :ROWS] - 2.0
    cross = columns_of(suffix(SCALE * m * rq[0, :, :ROWS] * rq[1, :, :ROWS]))
    crosses = [spread(cross, level) for level in range(LEVELS)]
    ones = jnp.ones((LANES, LANES), BF)

    for side in range(2):
        base = (1 - side) * D
        if side == 0:
            arrive(near_queries)
        row = (SCALE * LOG2E) * rq[side]
        gain = SCALE * rq[side] * inverse[8 * side : 8 * side + 8, :]
        acc = tuple(jnp.zeros((8, CHUNK), F32) for _ in range(LEVELS))
        for part, norms in enumerate((n0, n1)):
            if side == 0:
                arrive((near_keys, far_keys)[part])
            rows = slice(part * KEYS, (part + 1) * KEYS)
            for level in range(LEVELS):
                wide[level, rows, :] = spread(norms[side], level)
            raw_scores(ks.at[rows, :], xs, dots.at[part], side)

            def body(t, acc):
                at = pl.ds(pl.multiple_of(t * STEP_B, STEP_B), STEP_B)
                to = pl.ds(pl.multiple_of(part * KEYS + t * STEP_B, STEP_B), STEP_B)
                dot = jnp.zeros((STEP_B, CHUNK), F32)
                sums = []
                for level in range(LEVELS):
                    dot = dot + dots[part, level, at, :]
                    key = widen(wide[level, to, :], CHUNK // LANES)
                    scaled = dot * key
                    grow = jnp.exp2(scaled * row[level : level + 1, :])
                    weight = grow * gain[level : level + 1, :]
                    ws[level, to, :] = (weight * key).astype(BF)
                    pa = weight * scaled
                    sums.append(acc[level] + fold(pa))
                    summed = pa[:, :LANES]
                    for b in range(1, CHUNK // LANES):
                        summed = summed + pa[:, b * LANES : (b + 1) * LANES]
                    ea[level, to, :] = summed
                return tuple(sums)

            acc = lax.fori_loop(0, KEYS // STEP_B, body, acc, unroll=True)

        ebs = [None] * LEVELS
        held = None
        for level in range(LEVELS - 1, -1, -1):
            term = sums_down(ea[level], ones) * wide[level] * wide[level]
            held = term if held is None else held + term
            ebs[level] = held
        for lower, upper in ((0, 128), (128, 256), (256, 512), (512, 1024)):
            grad = None
            for level in range(2 if lower == 0 else EDGES.index(lower), LEVELS):
                more = dot_nn(ws[level], xs[side, :, lower:upper])
                grad = more if grad is None else grad + more
            if lower == 0:
                for level in (1, 0):
                    more = dot_nn(ws[level], xs[side, :, lower:upper])
                    grad = grad + jnp.where(iota((BANK, LANES), 1) < EDGES[level + 1], more, 0.0)
            for block in range(lower // LANES, upper // LANES):
                rel = slice(block * LANES - lower, (block + 1) * LANES - lower)
                home = slice(base + block * LANES, base + (block + 1) * LANES)
                value = grad[:, rel] - pick(ebs, block) * ks[:, home].astype(F32)
                gown[:, home] = value[:KEYS]
                gother[:KEYS, home] = value[KEYS:].astype(BF)
        leave(4, slice(0, KEYS), slice(base, base + D))
        leave(5, slice(0, KEYS + 16), slice(base, base + D))

        rows = [jnp.sum(a, axis=0, keepdims=True) for a in acc]
        if side == 0:
            arrive(other_queries)
        ca = jnp.concatenate(rows + [jnp.zeros((2, CHUNK), F32)], axis=0)
        ca = jnp.concatenate([ca[:, :ROWS] + m * own, ca[:, ROWS:]], axis=1)
        ca = columns_of(suffix(ca * rq[side] * rq[side]))
        cas = [spread(ca, level) for level in range(LEVELS)]
        for level in range(LEVELS - 1, -1, -1):
            width = max(EDGES[level + 1], LANES)
            more = dot_tn(ws[level], ks[:, base : base + width])
            if level < 2:
                more = jnp.where(iota((CHUNK, LANES), 1) < EDGES[level + 1], more, 0.0)
            acc_q[:, :width] = more if level == LEVELS - 1 else acc_q[:, :width] + more
        place = slice(side * ROWS, (side + 1) * ROWS)
        for block in range(D // LANES):
            at = slice(block * LANES, (block + 1) * LANES)
            value = acc_q[:, at] - pick(cas, block) * xs[side, :, at].astype(F32)
            partner = xs[1 - side, :ROWS, at].astype(F32)
            gq0[place, at] = value[:ROWS] + pick(crosses, block) * partner
            for s, ref in ((1, gq1), (2, gq2), (3, gq3)):
                ref[place, at] = value[s * ROWS : (s + 1) * ROWS].astype(BF)
        for n in range(RING):
            leave(n, place, slice(0, D))
    arrive(leaving)


def after_core(own, other, loss, kept, y1, y2, y3):
    tail = other[KEYS:, :LANES].astype(F32)[:8]
    total = loss[...] + jnp.broadcast_to(jnp.sum(tail, axis=1, keepdims=True), (8, LANES))
    for s, ref in enumerate((kept, y1, y2, y3)):
        rows = slice(s * NEAR, (s + 1) * NEAR)
        ref[:, : 2 * D] = (own[rows, :] + other[rows, :].astype(F32)).astype(ref.dtype)
        put_loss(ref, total)


def after_y(own, r1, r2, r3, *rest):
    send = rest[-1]
    for at in range(0, 2 * D, LANES):
        cols = slice(at, at + LANES)
        value = own[:, cols] + r1[:, cols].astype(F32)
        send[:, cols] = (value + (r2[:, cols].astype(F32) + r3[:, cols].astype(F32))).astype(BF)
    put_loss(send, (loss_of(own) + loss_of(r1)) + (loss_of(r2) + loss_of(r3)))


def at_end(got, after, image_bank, text_bank, losses):
    for at in range(0, 2 * D, 2 * LANES):
        value = fold(got[:, at : at + 2 * LANES].astype(F32))
        if at < D:
            image_bank[:, at : at + 2 * LANES] = value
        else:
            text_bank[:, at - D : at - D + 2 * LANES] = value
    tail = fold(got[:, 2 * D :].astype(F32)) * (1.0 / 65536.0)
    for level in range(LEVELS):
        losses[level] = jnp.sum(tail[level : level + 1, :])


def query_end(own, r1, r2, r3, grad_image, grad_text):
    for kind, ref in ((0, grad_image), (1, grad_text)):
        rows = slice(kind * ROWS, (kind + 1) * ROWS)
        value = own[rows, :] + r1[rows, :].astype(F32)
        ref[...] = value + (r2[rows, :].astype(F32) + r3[rows, :].astype(F32))


def shaped(shape, dtype=F32):
    return jax.ShapeDtypeStruct(shape, dtype)


def call(kernel, outs, scratch=()):
    return pl.pallas_call(
        kernel,
        out_shape=tuple(outs),
        scratch_shapes=tuple(scratch),
        compiler_params=pltpu.CompilerParams(vmem_limit_bytes=VMEM_LIMIT),
    )


def move(value, step, flip=0):
    pairs = []
    for i in range(2 * RING):
        x, c = divmod(i, 2)
        pairs.append((i, 2 * ((x + step) % RING) + (c ^ flip)))
    return lax.ppermute(value, ("x", "c"), pairs)


def along_y(value, step):
    n = lax.axis_size("y")
    return lax.ppermute(value, "y", [(i, (i + step) % n) for i in range(n)])


def exchange(value):
    return lax.all_to_all(value, "z", 0, 0, tiled=True)


ANYWHERE = pl.BlockSpec(memory_space=pl.ANY)
INSIDE = pl.BlockSpec(memory_space=pltpu.VMEM)


def placed(kernel, ins, outs, shapes, scratch=()):
    return pl.pallas_call(
        kernel,
        out_shape=tuple(shapes),
        in_specs=list(ins),
        out_specs=tuple(outs),
        scratch_shapes=tuple(scratch),
        compiler_params=pltpu.CompilerParams(vmem_limit_bytes=VMEM_LIMIT),
    )


def on_device(image, text, image_bank, text_bank):
    query = jnp.concatenate([image, text], axis=0)
    up, down = move(query, 1), move(query, -1)
    queries = [query, up, move(up[:ROWS], 1), move(down[ROWS:], -1), down]
    bank = jnp.concatenate([image_bank, text_bank], axis=1)
    near = exchange(jnp.tile(bank, (PAIRS, 1)))
    around = [near] + [along_y(near, s) for s in (1, 2, 3)]
    rq, matched = call(prepare, [shaped((2, 8, CHUNK)), shaped((8, ROWS))])(*queries)
    (n0,) = placed(prepare_keys, [INSIDE] * 4 + [ANYWHERE], [INSIDE], [shaped((2, KEYS, LANES))])(*around, matched)
    n1 = move(n0, 0, 1)
    far = [move(b, 0, 1) for b in around]
    blocks = queries + around + far
    held = [
        pltpu.VMEM((2, CHUNK, D), BF),
        pltpu.VMEM((BANK, 2 * D), BF),
    ]
    scores = [pltpu.VMEM((2, LEVELS, KEYS, CHUNK), F32), pltpu.VMEM((LEVELS, BANK, LANES), F32)]

    (sums,) = placed(
        forward,
        [ANYWHERE] * 13 + [INSIDE] * 4,
        [INSIDE],
        [shaped((16, CHUNK))],
        held + scores + [pltpu.SemaphoreType.DMA((16,))],
    )(*blocks, rq, matched, n0, n1)
    found = [sums] + [move(sums, s) for s in (1, 2, 3)]
    grads = [
        shaped((2 * ROWS, D)),
        shaped((2 * ROWS, D), BF),
        shaped((2 * ROWS, D), BF),
        shaped((2 * ROWS, D), BF),
        shaped((KEYS, 2 * D)),
        shaped((KEYS + 16, 2 * D), BF),
    ]
    gq0, gq1, gq2, gq3, gown, gother, loss = placed(
        backward,
        [ANYWHERE] * 13 + [INSIDE] * 8,
        [ANYWHERE] * 6 + [INSIDE],
        grads + [shaped((8, LANES))],
        held
        + [pltpu.VMEM(g.shape, g.dtype) for g in grads]
        + scores
        + [
            pltpu.VMEM((LEVELS, BANK, CHUNK), BF),
            pltpu.VMEM((LEVELS, BANK, LANES), F32),
            pltpu.VMEM((CHUNK, D), F32),
            pltpu.SemaphoreType.DMA((16,)),
            pltpu.SemaphoreType.DMA((12,)),
        ],
    )(*blocks, rq, matched, n0, n1, *found)

    back = [move(g, -s) for s, g in ((1, gq1), (2, gq2), (3, gq3))]
    kept, y1, y2, y3 = call(
        after_core,
        [shaped((NEAR, 2 * D + LANES))] + [shaped((NEAR, 2 * D + LANES), BF)] * 3,
    )(gown, move(gother, 0, 1), loss)
    summed = [along_y(g, -s) for s, g in ((1, y1), (2, y2), (3, y3))]
    (send,) = placed(
        after_y, [INSIDE] * 4 + [ANYWHERE] * 1, [INSIDE], [shaped((NEAR, 2 * D + LANES), BF)]
    )(kept, *summed, back[0])
    got = exchange(send)
    grad_image, grad_text = call(query_end, [shaped((ROWS, D))] * 2)(gq0, *back)
    grad_image_bank, grad_text_bank, losses = placed(
        at_end,
        [INSIDE, ANYWHERE],
        [INSIDE, INSIDE, pl.BlockSpec(memory_space=pltpu.SMEM)],
        [shaped((8, D)), shaped((8, D)), shaped((LEVELS,))],
    )(got, grad_image)
    return losses, grad_image, grad_text, grad_image_bank, grad_text_bank


def solution(mesh):
    torus = Mesh(mesh.devices.reshape(4, 8, 4, 2), ("y", "z", "x", "c"))
    rows = P(("y", "z", "x", "c"), None)
    return jax.shard_map(
        on_device,
        mesh=torus,
        in_specs=(rows,) * 4,
        out_specs=(P(),) + (rows,) * 4,
        check_vma=False,
    )
```

```python
import jax
import jax.numpy as jnp
from jax import lax
from jax.experimental import pallas as pl
from jax.experimental.pallas import tpu as pltpu
from jax.sharding import Mesh, PartitionSpec as P

SCALE = 20.0
EPS = 1e-06
LOG2E = 1.4426950408889634
LEVELS = 6
EDGES = (0, 32, 64, 128, 256, 512, 1024)
D = 1024
ROWS = 128
RING = 4
CHUNK = ROWS * RING
KEYS = 256
BANK = 2 * KEYS
LANES = 128
PAIRS = 8
NEAR = 64
STEP_F = 32
STEP_B = 32
VMEM_LIMIT = 56 * 1024 * 1024
BF = jnp.bfloat16
F32 = jnp.float32


def dot_nt(left, right):
    return lax.dot_general(left, right, (((1,), (1,)), ((), ())), preferred_element_type=F32)


def dot_nn(left, right):
    return lax.dot_general(left, right, (((1,), (0,)), ((), ())), preferred_element_type=F32)


def dot_tn(left, right):
    return lax.dot_general(left, right, (((0,), (0,)), ((), ())), preferred_element_type=F32)


def iota(shape, axis):
    return lax.broadcasted_iota(jnp.int32, shape, axis)


def level_mask(shape, level_axis):
    width = jnp.left_shift(32, jnp.minimum(iota(shape, level_axis), LEVELS - 1))
    return jnp.where(iota(shape, 1 - level_axis) < width, 1.0, 0.0).astype(BF)


def halves(values):
    high = values.astype(BF)
    return high, (values - high.astype(F32)).astype(BF)


def sums_across(values, mask):
    high, low = halves(values)
    return dot_nt(mask, high) + dot_nt(mask, low)


def sums_down(values, mask):
    high, low = halves(values)
    return dot_nn(high, mask) + dot_nn(low, mask)


def pick_lanes(values, level):
    lane = iota(values.shape, 1)
    keep = (lane >= EDGES[level]) & (lane < EDGES[level + 1])
    return jnp.where(keep, values.astype(F32), 0.0).astype(BF)


def keys_of(keys, side):
    return slice((1 - side) * D, (2 - side) * D)


def raw_scores(keys, queries, dots, side):
    base = (1 - side) * D
    for level in range(3):
        dots[level] = dot_nt(keys[:, base : base + LANES], pick_lanes(queries[side, :, :LANES], level))
    for level in range(3, LEVELS):
        lower, upper = EDGES[level], EDGES[level + 1]
        dots[level] = dot_nt(keys[:, base + lower : base + upper], queries[side, :, lower:upper])


def fold(values):
    return jnp.sum(values.reshape(values.shape[0] // 8, 8, values.shape[1]), axis=0)


def widen(values, n):
    return jnp.concatenate([values] * n, axis=1)


def spread(cols, level):
    return jnp.broadcast_to(cols[:, level : level + 1], (cols.shape[0], LANES))


def prepare(q0, q1, q2a, q2b, q3, rq, matched):
    across = level_mask((16, D), 0)
    for side in range(2):
        rows = slice(side * ROWS, (side + 1) * ROWS)
        for s, block in enumerate((q0[rows, :], q1[rows, :], (q2a, q2b)[side][...], q3[rows, :])):
            wide = block.astype(F32)
            found = lax.rsqrt(sums_across(wide * wide, across) + EPS)
            rq[side, :, s * ROWS : (s + 1) * ROWS] = found[:8]
    product = q0[:ROWS, :].astype(F32) * q0[ROWS:, :].astype(F32)
    matched[...] = SCALE * sums_across(product, across)[:8] * rq[0, :, :ROWS] * rq[1, :, :ROWS]


def prepare_keys(b0, b1, b2, b3, after, later, kn):
    down = level_mask((D, LANES), 1)
    for s, block in enumerate((b0, b1, b2, b3)):
        for side in range(2):
            y = block[:, keys_of(block, side)].astype(F32)
            kn[side, s * NEAR : (s + 1) * NEAR, :] = lax.rsqrt(sums_down(y * y, down) + EPS)


def fetch(blocks, xs, ks, sems):
    q0, q1, q2a, q2b, q3 = blocks[:5]
    count = 0

    def start(source, target):
        nonlocal count
        copy = pltpu.make_async_copy(source, target, sems.at[count])
        copy.start()
        count += 1
        return copy

    def queries(side):
        rows = slice(side * ROWS, (side + 1) * ROWS)
        parts = (q0.at[rows, :], q1.at[rows, :], (q2a, q2b)[side], q3.at[rows, :])
        return [start(p, xs.at[side, s * ROWS : (s + 1) * ROWS, :]) for s, p in enumerate(parts)]

    def keys(part):
        found = blocks[5 + 4 * part : 9 + 4 * part]
        return [start(b, ks.at[part * KEYS + s * NEAR : part * KEYS + (s + 1) * NEAR, :]) for s, b in enumerate(found)]

    first = queries(0)
    return [first, keys(0), keys(1), queries(1)]


def arrive(copies):
    for copy in copies:
        copy.wait()


def forward(*refs):
    rq, matched, n0, n1 = refs[13:17]
    sums, xs, ks, dots, wide, sems = refs[17:]
    near_queries, near_keys, far_keys, other_queries = fetch(refs[:13], xs, ks, sems)
    grown = jnp.exp(matched[...])
    total = jnp.broadcast_to(jnp.sum(matched[...], axis=1, keepdims=True), (8, ROWS))
    spare = [jnp.concatenate([total[r : r + 1] for r in rows], axis=1) for rows in ((0, 1, 2, 3), (4, 5, 5, 5))]
    for side in range(2):
        row = (SCALE * LOG2E) * rq[side]
        arrive(near_queries if side == 0 else other_queries)
        acc = tuple(jnp.zeros((8, CHUNK), F32) for _ in range(LEVELS))
        for part, norms in enumerate((n0, n1)):
            if side == 0:
                arrive((near_keys, far_keys)[part])
            rows = slice(part * KEYS, (part + 1) * KEYS)
            for level in range(LEVELS):
                wide[level, rows, :] = spread(norms[side], level)
            raw_scores(ks.at[rows, :], xs, dots.at[part], side)

            def body(t, acc):
                at = pl.ds(pl.multiple_of(t * STEP_F, STEP_F), STEP_F)
                to = pl.ds(pl.multiple_of(part * KEYS + t * STEP_F, STEP_F), STEP_F)
                dot = jnp.zeros((STEP_F, CHUNK), F32)
                out = []
                for level in range(LEVELS):
                    dot = dot + dots[part, level, at, :]
                    key = widen(wide[level, to, :], CHUNK // LANES)
                    grow = jnp.exp2(dot * key * row[level : level + 1, :])
                    out.append(acc[level] + fold(grow))
                return tuple(out)

            acc = lax.fori_loop(0, KEYS // STEP_F, body, acc, unroll=True)
        rows = [jnp.sum(a, axis=0, keepdims=True) for a in acc]
        sums[8 * side : 8 * side + 8, :] = jnp.concatenate(rows + spare, axis=0)
        sums[8 * side : 8 * side + LEVELS, :ROWS] = sums[8 * side : 8 * side + LEVELS, :ROWS] + grown[:LEVELS]


def suffix(rows):
    out = [rows[LEVELS - 1 : LEVELS]]
    for level in range(LEVELS - 2, -1, -1):
        out.append(out[-1] + rows[level : level + 1])
    return jnp.concatenate(out[::-1] + [jnp.zeros((2, rows.shape[1]), F32)], axis=0)


def columns_of(rows):
    n = rows.shape[1]
    return jnp.transpose(jnp.concatenate([rows, jnp.zeros((LANES - 8, n), F32)], axis=0))


def by_lane(parts):
    lane = iota(parts[0].shape, 1)
    return jnp.where(lane < EDGES[1], parts[0], jnp.where(lane < EDGES[2], parts[1], parts[2]))


def pick(parts, block):
    if block == 0:
        return by_lane(parts[:3])
    return parts[3 if block == 1 else (4 if block < 4 else 5)]


def put_loss(ref, loss):
    ref[:, 2 * D :] = jnp.concatenate([loss_tail(loss)] * (NEAR // 8), axis=0).astype(ref.dtype)


def loss_of(ref):
    tail = ref[:, 2 * D :].astype(F32)[:8]
    return jnp.broadcast_to(jnp.sum(tail, axis=1, keepdims=True), (8, LANES))


def loss_tail(loss):
    high = loss.astype(BF).astype(F32)
    mid = (loss - high).astype(BF).astype(F32)
    low = (loss - high) - mid
    lane = iota(loss.shape, 1)
    return jnp.where(lane == 0, high, jnp.where(lane == 1, mid, jnp.where(lane == 2, low, 0.0)))


def backward(*refs):
    rq, matched, n0, n1, s0, s1, s2, s3 = refs[13:21]
    outs, loss = refs[21:27], refs[27]
    xs, ks, gq0, gq1, gq2, gq3, gown, gother, dots, wide, ws, ea, acc_q, sems, out_sems = refs[28:]
    near_queries, near_keys, far_keys, other_queries = fetch(refs[:13], xs, ks, sems)
    leaving = []

    def leave(n, rows, cols):
        source = (gq0, gq1, gq2, gq3, gown, gother)[n]
        copy = pltpu.make_async_copy(source.at[rows, cols], outs[n].at[rows, cols], out_sems.at[len(leaving)])
        copy.start()
        leaving.append(copy)

    parts = (s0, s1, s2, s3)
    total = []
    for s in range(RING):
        found = None
        for t in range(RING):
            at = ((s - t) % RING) * ROWS
            more = parts[t][:, at : at + ROWS]
            found = more if found is None else found + more
        total.append(found)
    total = jnp.concatenate(total, axis=1)
    inverse = 1.0 / total
    logs = jnp.log(total)
    spare = (s0[6:8, :] + s1[6:8, :]) + (s2[6:8, :] + s3[6:8, :])
    all_matched = [spare[r // 4 : r // 4 + 1, (r % 4) * ROWS : (r % 4 + 1) * ROWS] for r in range(LEVELS)]
    all_matched = jnp.concatenate(all_matched + [jnp.zeros((2, ROWS), F32)], axis=0)
    each = jnp.sum(logs[:8] + logs[8:], axis=1, keepdims=True)
    mine = jnp.broadcast_to(each, (8, LANES)) - 2.0 * all_matched
    loss[...] = mine
    gother[KEYS:, :LANES] = jnp.concatenate([loss_tail(mine)] * 2, axis=0).astype(BF)
    gother[KEYS:, LANES:] = jnp.zeros((16, 2 * D - LANES), BF)

    own = matched[...]
    grown = jnp.exp(own)
    m = grown * inverse[:8, :ROWS] + grown * inverse[8:, :ROWS] - 2.0
    cross = columns_of(suffix(SCALE * m * rq[0, :, :ROWS] * rq[1, :, :ROWS]))
    crosses = [spread(cross, level) for level in range(LEVELS)]
    ones = jnp.ones((LANES, LANES), BF)

    for side in range(2):
        base = (1 - side) * D
        if side == 0:
            arrive(near_queries)
        row = (SCALE * LOG2E) * rq[side]
        gain = SCALE * rq[side] * inverse[8 * side : 8 * side + 8, :]
        acc = tuple(jnp.zeros((8, CHUNK), F32) for _ in range(LEVELS))
        for part, norms in enumerate((n0, n1)):
            if side == 0:
                arrive((near_keys, far_keys)[part])
            rows = slice(part * KEYS, (part + 1) * KEYS)
            for level in range(LEVELS):
                wide[level, rows, :] = spread(norms[side], level)
            raw_scores(ks.at[rows, :], xs, dots.at[part], side)

            def body(t, acc):
                at = pl.ds(pl.multiple_of(t * STEP_B, STEP_B), STEP_B)
                to = pl.ds(pl.multiple_of(part * KEYS + t * STEP_B, STEP_B), STEP_B)
                dot = jnp.zeros((STEP_B, CHUNK), F32)
                sums = []
                for level in range(LEVELS):
                    dot = dot + dots[part, level, at, :]
                    key = widen(wide[level, to, :], CHUNK // LANES)
                    scaled = dot * key
                    grow = jnp.exp2(scaled * row[level : level + 1, :])
                    weight = grow * gain[level : level + 1, :]
                    ws[level, to, :] = (weight * key).astype(BF)
                    pa = weight * scaled
                    sums.append(acc[level] + fold(pa))
                    summed = pa[:, :LANES]
                    for b in range(1, CHUNK // LANES):
                        summed = summed + pa[:, b * LANES : (b + 1) * LANES]
                    ea[level, to, :] = summed
                return tuple(sums)

            acc = lax.fori_loop(0, KEYS // STEP_B, body, acc, unroll=True)

        ebs = [None] * LEVELS
        held = None
        for level in range(LEVELS - 1, -1, -1):
            term = sums_down(ea[level], ones) * wide[level] * wide[level]
            held = term if held is None else held + term
            ebs[level] = held
        for lower, upper in ((0, 128), (128, 256), (256, 512), (512, 1024)):
            grad = None
            for level in range(2 if lower == 0 else EDGES.index(lower), LEVELS):
                more = dot_nn(ws[level], xs[side, :, lower:upper])
                grad = more if grad is None else grad + more
            if lower == 0:
                for level in (1, 0):
                    more = dot_nn(ws[level], xs[side, :, lower:upper])
                    grad = grad + jnp.where(iota((BANK, LANES), 1) < EDGES[level + 1], more, 0.0)
            for block in range(lower // LANES, upper // LANES):
                rel = slice(block * LANES - lower, (block + 1) * LANES - lower)
                home = slice(base + block * LANES, base + (block + 1) * LANES)
                value = grad[:, rel] - pick(ebs, block) * ks[:, home].astype(F32)
                gown[:, home] = value[:KEYS]
                gother[:KEYS, home] = value[KEYS:].astype(BF)
        leave(4, slice(0, KEYS), slice(base, base + D))
        leave(5, slice(0, KEYS + 16), slice(base, base + D))

        rows = [jnp.sum(a, axis=0, keepdims=True) for a in acc]
        if side == 0:
            arrive(other_queries)
        ca = jnp.concatenate(rows + [jnp.zeros((2, CHUNK), F32)], axis=0)
        ca = jnp.concatenate([ca[:, :ROWS] + m * own, ca[:, ROWS:]], axis=1)
        ca = columns_of(suffix(ca * rq[side] * rq[side]))
        cas = [spread(ca, level) for level in range(LEVELS)]
        for level in range(LEVELS - 1, -1, -1):
            width = max(EDGES[level + 1], LANES)
            more = dot_tn(ws[level], ks[:, base : base + width])
            if level < 2:
                more = jnp.where(iota((CHUNK, LANES), 1) < EDGES[level + 1], more, 0.0)
            acc_q[:, :width] = more if level == LEVELS - 1 else acc_q[:, :width] + more
        place = slice(side * ROWS, (side + 1) * ROWS)
        for block in range(D // LANES):
            at = slice(block * LANES, (block + 1) * LANES)
            value = acc_q[:, at] - pick(cas, block) * xs[side, :, at].astype(F32)
            partner = xs[1 - side, :ROWS, at].astype(F32)
            gq0[place, at] = value[:ROWS] + pick(crosses, block) * partner
            for s, ref in ((1, gq1), (2, gq2), (3, gq3)):
                ref[place, at] = value[s * ROWS : (s + 1) * ROWS].astype(BF)
        for n in range(RING):
            leave(n, place, slice(0, D))
    arrive(leaving)


def after_core(own, other, loss, kept, y1, y2, y3):
    tail = other[KEYS:, :LANES].astype(F32)[:8]
    total = loss[...] + jnp.broadcast_to(jnp.sum(tail, axis=1, keepdims=True), (8, LANES))
    for s, ref in enumerate((kept, y1, y2, y3)):
        rows = slice(s * NEAR, (s + 1) * NEAR)
        ref[:, : 2 * D] = (own[rows, :] + other[rows, :].astype(F32)).astype(ref.dtype)
        put_loss(ref, total)


def after_y(own, r1, r2, r3, *rest):
    send = rest[-1]
    for at in range(0, 2 * D, LANES):
        cols = slice(at, at + LANES)
        value = own[:, cols] + r1[:, cols].astype(F32)
        send[:, cols] = (value + (r2[:, cols].astype(F32) + r3[:, cols].astype(F32))).astype(BF)
    put_loss(send, (loss_of(own) + loss_of(r1)) + (loss_of(r2) + loss_of(r3)))


def at_end(got, after, image_bank, text_bank, losses):
    for at in range(0, 2 * D, 2 * LANES):
        value = fold(got[:, at : at + 2 * LANES].astype(F32))
        if at < D:
            image_bank[:, at : at + 2 * LANES] = value
        else:
            text_bank[:, at - D : at - D + 2 * LANES] = value
    tail = fold(got[:, 2 * D :].astype(F32)) * (1.0 / 65536.0)
    for level in range(LEVELS):
        losses[level] = jnp.sum(tail[level : level + 1, :])


def query_end(own, r1, r2, r3, grad_image, grad_text):
    for kind, ref in ((0, grad_image), (1, grad_text)):
        rows = slice(kind * ROWS, (kind + 1) * ROWS)
        value = own[rows, :] + r1[rows, :].astype(F32)
        ref[...] = value + (r2[rows, :].astype(F32) + r3[rows, :].astype(F32))


def shaped(shape, dtype=F32):
    return jax.ShapeDtypeStruct(shape, dtype)


def call(kernel, outs, scratch=()):
    return pl.pallas_call(
        kernel,
        out_shape=tuple(outs),
        scratch_shapes=tuple(scratch),
        compiler_params=pltpu.CompilerParams(vmem_limit_bytes=VMEM_LIMIT),
    )


def move(value, step, flip=0):
    pairs = []
    for i in range(2 * RING):
        x, c = divmod(i, 2)
        pairs.append((i, 2 * ((x + step) % RING) + (c ^ flip)))
    return lax.ppermute(value, ("x", "c"), pairs)


def along_y(value, step):
    n = lax.axis_size("y")
    return lax.ppermute(value, "y", [(i, (i + step) % n) for i in range(n)])


def exchange(value):
    return lax.all_to_all(value, "z", 0, 0, tiled=True)


ANYWHERE = pl.BlockSpec(memory_space=pl.ANY)
INSIDE = pl.BlockSpec(memory_space=pltpu.VMEM)


def placed(kernel, ins, outs, shapes, scratch=()):
    return pl.pallas_call(
        kernel,
        out_shape=tuple(shapes),
        in_specs=list(ins),
        out_specs=tuple(outs),
        scratch_shapes=tuple(scratch),
        compiler_params=pltpu.CompilerParams(vmem_limit_bytes=VMEM_LIMIT),
    )


def on_device(image, text, image_bank, text_bank):
    query = jnp.concatenate([image, text], axis=0)
    up, down = move(query, 1), move(query, -1)
    queries = [query, up, move(up[:ROWS], 1), move(down[ROWS:], -1), down]
    bank = jnp.concatenate([image_bank, text_bank], axis=1)
    near = exchange(jnp.tile(bank, (PAIRS, 1)))
    around = [near] + [along_y(near, s) for s in (1, 2, 3)]
    rq, matched = call(prepare, [shaped((2, 8, CHUNK)), shaped((8, ROWS))])(*queries)
    (n0,) = placed(prepare_keys, [INSIDE] * 4 + [ANYWHERE] * 2, [INSIDE], [shaped((2, KEYS, LANES))])(
        *around, queries[2], queries[3]
    )
    n1 = move(n0, 0, 1)
    far = [move(b, 0, 1) for b in around]
    blocks = queries + around + far
    held = [
        pltpu.VMEM((2, CHUNK, D), BF),
        pltpu.VMEM((BANK, 2 * D), BF),
    ]
    scores = [pltpu.VMEM((2, LEVELS, KEYS, CHUNK), F32), pltpu.VMEM((LEVELS, BANK, LANES), F32)]

    (sums,) = placed(
        forward,
        [ANYWHERE] * 13 + [INSIDE] * 4,
        [INSIDE],
        [shaped((16, CHUNK))],
        held + scores + [pltpu.SemaphoreType.DMA((16,))],
    )(*blocks, rq, matched, n0, n1)
    found = [sums] + [move(sums, s) for s in (1, 2, 3)]
    grads = [
        shaped((2 * ROWS, D)),
        shaped((2 * ROWS, D), BF),
        shaped((2 * ROWS, D), BF),
        shaped((2 * ROWS, D), BF),
        shaped((KEYS, 2 * D)),
        shaped((KEYS + 16, 2 * D), BF),
    ]
    gq0, gq1, gq2, gq3, gown, gother, loss = placed(
        backward,
        [ANYWHERE] * 13 + [INSIDE] * 8,
        [ANYWHERE] * 6 + [INSIDE],
        grads + [shaped((8, LANES))],
        held
        + [pltpu.VMEM(g.shape, g.dtype) for g in grads]
        + scores
        + [
            pltpu.VMEM((LEVELS, BANK, CHUNK), BF),
            pltpu.VMEM((LEVELS, BANK, LANES), F32),
            pltpu.VMEM((CHUNK, D), F32),
            pltpu.SemaphoreType.DMA((16,)),
            pltpu.SemaphoreType.DMA((12,)),
        ],
    )(*blocks, rq, matched, n0, n1, *found)

    back = [move(g, -s) for s, g in ((1, gq1), (2, gq2), (3, gq3))]
    kept, y1, y2, y3 = call(
        after_core,
        [shaped((NEAR, 2 * D + LANES))] + [shaped((NEAR, 2 * D + LANES), BF)] * 3,
    )(gown, move(gother, 0, 1), loss)
    summed = [along_y(g, -s) for s, g in ((1, y1), (2, y2), (3, y3))]
    (send,) = placed(
        after_y, [INSIDE] * 4 + [ANYWHERE] * 1, [INSIDE], [shaped((NEAR, 2 * D + LANES), BF)]
    )(kept, *summed, back[0])
    got = exchange(send)
    grad_image, grad_text = call(query_end, [shaped((ROWS, D))] * 2)(gq0, *back)
    grad_image_bank, grad_text_bank, losses = placed(
        at_end,
        [INSIDE, ANYWHERE],
        [INSIDE, INSIDE, pl.BlockSpec(memory_space=pltpu.SMEM)],
        [shaped((8, D)), shaped((8, D)), shaped((LEVELS,))],
    )(got, grad_image)
    return losses, grad_image, grad_text, grad_image_bank, grad_text_bank


def solution(mesh):
    torus = Mesh(mesh.devices.reshape(4, 8, 4, 2), ("y", "z", "x", "c"))
    rows = P(("y", "z", "x", "c"), None)
    return jax.shard_map(
        on_device,
        mesh=torus,
        in_specs=(rows,) * 4,
        out_specs=(P(),) + (rows,) * 4,
        check_vma=False,
    )
```
